32 devices in a mesh: replica: 4 (over y, core), fsdp: 8 (over z, x).
Axes of the slice: x: 2, y: 2, z: 4, core: 2. Of those that a mesh axis runs over, the one named last changes fastest.
Arguments:
- tokens_in: bfloat16 [4, 3072, 8192], P('replica', 'fsdp'), may hold values from -6 to 6
- targets: bfloat16 [4, 3072, 512], P('replica', 'fsdp'), may hold values from -6 to 6
- weights: float32 [4, 8192, 512], P('replica', 'fsdp'), may hold values from -6 to 6
- adam_mean: float32 [4, 8192, 512], P('replica', 'fsdp'), may hold values from -6 to 6
- adam_var: float32 [4, 8192, 512], P('replica', 'fsdp'), may hold values from 0.5 to 8
- anchor: float32 [8192, 512], P('fsdp'), may hold values from -6 to 6
- outer_momentum: float32 [8192, 512], P('fsdp'), may hold values from -6 to 6
- pseudo_grad: float32 [4, 8192, 128], P('replica', 'fsdp'), may hold values from -6 to 6
- fragment: int32 [], replicated, may hold values from 0 to 3
- delay: int32 [4], P('replica'), may hold values from 0 to 1, as said below
Outputs:
- new_weights: float32 [4, 8192, 512], P('replica', 'fsdp')
- new_adam_mean: float32 [4, 8192, 512], P('replica', 'fsdp')
- new_adam_var: float32 [4, 8192, 512], P('replica', 'fsdp')
- new_anchor: float32 [8192, 512], P('fsdp')
- new_momentum: float32 [8192, 512], P('fsdp')
The draws below stay inside these ranges and needn't reach their ends.
Inputs may be any that keep to these rules, and one draw needn't show every extreme that they name: Exactly 2 of the workers have delay 1, the others 0.
All inputs are finite; a program needn't handle non-finite values.
Results may differ from the reference program's by a relative error of at most 0.00053.
Values may be sent and summed in bfloat16 or wider, within the bound.
A program may use at most 128 MiB of HBM per device.

```python
import math
import jax
import jax.numpy as jnp
from jax import lax

D = 8192
KW = 512
HEAD = 128
TOKENS = 3072
WORKERS = 4
N_REPLICA = 4


def draw_delay(key, part):
    key = jax.random.fold_in(key, 5)
    order = jax.random.permutation(key, WORKERS)
    return (order < WORKERS // 2).astype(jnp.int32)


def strengthened(values, stream_key, source, target, blocks, factor):
    owner, partner = [(jnp.arange(values.shape[dim]) // (values.shape[dim] // blocks)).reshape([-1 if axis == dim else 1 for axis in range(values.ndim)]) for dim in (source, target)]
    chosen = jax.random.permutation(stream_key, blocks)[partner]
    strong = (owner == chosen) | (owner == (partner + blocks // 2) % blocks)
    return jnp.where(strong, factor * values, values)


def shard_levels(own_key, extent, pieces, smallest, largest):
    def one(position, shards_of):
        steps = jax.random.uniform(jax.random.fold_in(jax.random.fold_in(own_key, 6), position), (shards_of,), jnp.float32, smallest / len(pieces), largest / len(pieces))
        return jnp.repeat(jnp.exp(steps), extent[position] // shards_of).reshape((-1,) + (1,) * (len(extent) - position - 1))

    loudness = one(*pieces[0])
    for cut in pieces[1:]:
        loudness = loudness * one(*cut)
    return loudness


def normal_values(rng, extent, scale, limit, split=(), dtype=jnp.bfloat16):
    gain = shard_levels(rng, extent, split, -0.22, 0.18) if split else 1.0
    drawn = jax.random.normal(rng, extent, jnp.float32) * scale * gain
    return jnp.minimum(jnp.maximum(drawn, -limit), limit).astype(dtype)


def heavy_noise(stream_key, shape, spread, reach, split, heavy, held_as=jnp.bfloat16):
    values = spread * jax.random.normal(stream_key, shape, jnp.float32)
    if split:
        values = values * shard_levels(stream_key, shape, split, -0.22, 0.18)
    return jnp.clip(strengthened(values, jax.random.fold_in(stream_key, 3), *heavy), -reach, reach).astype(held_as)


def setup_inputs(seed: int = 0) -> dict:
    streams_of = jax.random.split(jax.random.key(seed), 11)
    tokens_in = heavy_noise(streams_of[0], (WORKERS, TOKENS, D), 1.0, 6.0, ((0, 4), (1, 8)), (1, 2, 8, 2.0))
    targets = normal_values(streams_of[1], (WORKERS, TOKENS, KW), 1.0, 6.0, ((0, 4), (1, 8)))
    weights = normal_values(streams_of[2], (WORKERS, D, KW), 1.0, 6.0, ((0, 4), (1, 8)), jnp.float32)
    adam_mean = normal_values(streams_of[3], (WORKERS, D, KW), 1.5, 6.0, ((0, 4), (1, 8)), jnp.float32)
    adam_var = jnp.clip(jnp.exp(math.log(8.0) - 2.7725887 * jax.random.uniform(streams_of[4], (WORKERS, D, KW), jnp.float32) ** shard_levels(streams_of[4], (WORKERS, D, KW), ((0, 4), (1, 8)), -0.2, 0.2)), 0.5, 8.0)
    anchor = normal_values(streams_of[5], (D, KW), 1.0, 6.0, ((0, 8),), jnp.float32)
    outer_momentum = normal_values(streams_of[6], (D, KW), 0.5, 6.0, ((0, 8),), jnp.float32)
    pseudo_grad = normal_values(streams_of[7], (WORKERS, D, HEAD), 0.5, 6.0, ((0, 4), (1, 8)), jnp.float32)
    fragment = jax.random.randint(streams_of[8], (), 0, KW // HEAD).astype(jnp.int32)
    delay = draw_delay(jax.random.fold_in(streams_of[10], 71), 0)
    return {"tokens_in": tokens_in, "targets": targets, "weights": weights, "adam_mean": adam_mean, "adam_var": adam_var, "anchor": anchor, "outer_momentum": outer_momentum, "pseudo_grad": pseudo_grad, "fragment": fragment, "delay": delay}


beta_first = 0.9
beta_second = 0.95
adam_epsilon = 1e-08
adam_steps = 20.0
inner_rate = 0.1
weight_decay = 0.1
outer_rate = 0.7
outer_pull = 0.9
blend_share = 0.5
norm_epsilon = 1e-05

def blend(field, anchor_next, offset):
    piece = lax.dynamic_slice_in_dim(field, offset, anchor_next.shape[1], 1)
    mixed = blend_share * anchor_next + (1.0 - blend_share) * piece
    return lax.dynamic_update_slice_in_dim(field, mixed, offset, 1)

def normalize(rows):
    wide = rows.astype(jnp.float32)
    stat = lax.optimization_barrier(jnp.mean(wide * wide, axis=-1, keepdims=True))
    return (wide * lax.rsqrt(stat + norm_epsilon)).astype(jnp.bfloat16)

def adam_update(start_field, grad, first, second):
    mean_next = beta_first * first + (1.0 - beta_first) * grad
    var_next = beta_second * second + (1.0 - beta_second) * grad * grad
    first_fix = 1.0 - beta_first ** adam_steps
    second_fix = 1.0 - beta_second ** adam_steps
    ratio = mean_next / first_fix / (jnp.sqrt(var_next / second_fix) + adam_epsilon)
    return (start_field - inner_rate * (ratio + weight_decay * start_field), mean_next, var_next)

def reference(tokens_in, targets, weights, adam_mean, adam_var, anchor, outer_momentum, pseudo_grad, fragment, delay):
    average = lax.optimization_barrier(jnp.sum(pseudo_grad, axis=0)) / N_REPLICA
    offset = (fragment * HEAD).astype(jnp.int32)
    anchor_piece = lax.dynamic_slice_in_dim(anchor, offset, HEAD, 1)
    moment_piece = lax.dynamic_slice_in_dim(outer_momentum, offset, HEAD, 1)
    moment_next = outer_pull * moment_piece + average
    anchor_next = anchor_piece - outer_rate * (average + outer_pull * moment_next)
    new_anchor = lax.dynamic_update_slice_in_dim(anchor, anchor_next, offset, 1)
    new_momentum = lax.dynamic_update_slice_in_dim(outer_momentum, moment_next, offset, 1)
    key_scale = 1.0 / math.sqrt(D)
    grad_scale = 1.0 / math.sqrt(TOKENS)
    results = []
    means = []
    variances = []
    for worker in range(N_REPLICA):
        local = weights[worker]
        flag = delay[worker]
        start_field = jnp.where(flag == 0, blend(local, anchor_next, offset), local)
        normed = normalize(tokens_in[worker])
        keys = jnp.dot(normed, start_field.astype(jnp.bfloat16), preferred_element_type=jnp.float32)
        residual = (keys * key_scale - targets[worker].astype(jnp.float32)).astype(jnp.bfloat16)
        grad = lax.dot_general(normed, residual, (((0,), (0,)), ((), ())), preferred_element_type=jnp.float32) * grad_scale
        stepped, mean_next, var_next = adam_update(start_field, grad, adam_mean[worker], adam_var[worker])
        results.append(jnp.where(flag == 1, blend(stepped, anchor_next, offset), stepped))
        means.append(mean_next)
        variances.append(var_next)
    return (jnp.stack(results), jnp.stack(means), jnp.stack(variances), new_anchor, new_momentum)
```

```python
import functools
import math

import jax
import jax.numpy as jnp
from jax import lax
from jax.experimental import pallas as pl
from jax.experimental.pallas import tpu as pltpu
from jax.sharding import PartitionSpec as P

beta_first = 0.9
beta_second = 0.95
adam_epsilon = 1e-08
adam_steps = 20.0
inner_rate = 0.1
weight_decay = 0.1
outer_rate = 0.7
outer_pull = 0.9
blend_share = 0.5
norm_epsilon = 1e-05

GROUP = 4
ROW_PARTS = 4
MESH = pl.DeviceIdType.MESH


def adam_update(start_field, grad, first, second):
    mean_next = beta_first * first + (1.0 - beta_first) * grad
    var_next = beta_second * second + (1.0 - beta_second) * grad * grad
    first_fix = 1.0 - beta_first**adam_steps
    second_fix = 1.0 - beta_second**adam_steps
    ratio = mean_next / first_fix / (jnp.sqrt(var_next / second_fix) + adam_epsilon)
    return (start_field - inner_rate * (ratio + weight_decay * start_field), mean_next, var_next)


def tile_of(extent, most):
    tile = min(extent, most)
    while extent % tile:
        tile //= 2
    return tile


def kernel(
    n_rep, n_fsdp,
    frag_ref, delay_ref, tokens_h, targets_h, weights_h, mean_h, var_h, anchor_h, moment_h, pg_h,
    weights_o, mean_o, var_o, anchor_o, moment_o,
    tin, tok, tgt, wf, wb, mean, var, anc, mom, pgs, kp, kin, rbuf, gbuf, gin,
    load_sem, tload_sem, out_sem,
    pg_ss, pg_rs, t_ss, t_rs, w_ss, w_rs, k_ss, k_rs, r_ss, r_rs, g_ss, g_rs,
):
    rows, width = tin.shape
    blk, kw = wf.shape
    head = pgs.shape[2]
    chunks = kw // head
    quads = n_fsdp // GROUP
    part = rows // ROW_PARTS
    me = lax.axis_index("fsdp")
    rep = lax.axis_index("replica")
    g = lax.rem(me, GROUP)
    q = lax.div(me, GROUP)

    def member(d):
        return lax.rem(g + d, GROUP)

    def quad(e):
        return lax.rem(q + e, quads)

    def to_member(d):
        return (rep, q * GROUP + member(d))

    def to_quad(e):
        return (rep, quad(e) * GROUP + g)

    def to_replica(d):
        return (lax.rem(rep + d, n_rep), me)

    def remote(src, dst, ss, rs, where):
        return pltpu.make_async_remote_copy(
            src_ref=src, dst_ref=dst, send_sem=ss, recv_sem=rs, device_id=where, device_id_type=MESH
        )

    loads = []
    for k in range(ROW_PARTS):
        span = pl.ds(k * part, part)
        loads.append(pltpu.make_async_copy(tokens_h.at[span], tin.at[span], tload_sem.at[k]))
        loads[-1].start()
    pairs = [
        (pg_h, pgs.at[rep]), (weights_h, wf), (anchor_h, anc), (moment_h, mom),
        (targets_h, tgt), (mean_h, mean), (var_h, var),
    ]
    more = []
    for i, (src, dst) in enumerate(pairs):
        more.append(pltpu.make_async_copy(src, dst, load_sem.at[i]))
        more[-1].start()

    peers = [to_replica(d) for d in range(1, n_rep)]
    peers += [to_member(d) for d in range(1, GROUP)]
    peers += [to_quad(e) for e in range(1, quads)]
    barrier = pltpu.get_barrier_semaphore()
    for where in peers:
        pl.semaphore_signal(barrier, inc=1, device_id=where, device_id_type=MESH)
    pl.semaphore_wait(barrier, len(peers))

    sent = []

    more[0].wait()
    pg_copies = []
    for d in range(1, n_rep):
        copy = remote(pgs.at[rep], pgs.at[rep], pg_ss.at[d - 1], pg_rs.at[d - 1], to_replica(d))
        copy.start()
        sent.append(copy)
        source = lax.rem(rep + n_rep - d, n_rep)
        pg_copies.append(
            remote(pgs.at[source], pgs.at[source], pg_ss.at[d - 1], pg_rs.at[d - 1], to_replica(d))
        )

    my_rows = pl.multiple_of(g * rows, 128)
    lane = 128
    for k in range(ROW_PARTS):
        loads[k].wait()

        def norm(i, _, k=k):
            at = pl.ds(pl.multiple_of(k * part + i * 16, 16), 16)
            total = jnp.zeros((16, lane), jnp.float32)
            for j in range(width // lane):
                v = tin[at, j * lane:(j + 1) * lane].astype(jnp.float32)
                total = total + v * v
            stat = jnp.sum(total, axis=-1, keepdims=True) * (1.0 / width)
            scale = jnp.broadcast_to(lax.rsqrt(stat + norm_epsilon), (16, lane))
            for j in range(width // lane):
                cols = slice(j * lane, (j + 1) * lane)
                tin[at, cols] = (tin[at, cols].astype(jnp.float32) * scale).astype(jnp.bfloat16)
            return 0

        lax.fori_loop(0, part // 16, norm, 0)
        span = pl.ds(k * part, part)
        dst_rows = pl.ds(pl.multiple_of(my_rows + k * part, 16), part)
        for d in range(1, GROUP):
            for j in range(quads):
                cols = pl.ds(pl.multiple_of((j * GROUP + member(d)) * blk, 128), blk)
                copy = remote(
                    tin.at[span, cols], tok.at[dst_rows, pl.ds(j * blk, blk)],
                    t_ss.at[k, d - 1, j], t_rs.at[k, d - 1, j], to_member(d),
                )
                copy.start()
                sent.append(copy)
        for j in range(quads):
            cols = pl.ds(pl.multiple_of((j * GROUP + g) * blk, 128), blk)
            tok[dst_rows, j * blk:(j + 1) * blk] = tin[span, cols]

    for copy in more[1:4]:
        copy.wait()
    for copy in pg_copies:
        copy.wait_recv()
    frag = frag_ref[0]
    flag = delay_ref[0]
    step_rows = tile_of(blk, 128)

    def outer(i, _):
        at = pl.ds(pl.multiple_of(i * step_rows, step_rows), step_rows)
        shape = (step_rows, head)
        total = pgs[0, at, :]
        for r in range(1, n_rep):
            total = total + pgs[r, at, :]
        average = total / n_rep
        frag_v = jnp.full(shape, frag, jnp.int32)
        flag_v = jnp.full(shape, flag, jnp.int32)
        for h in range(chunks):
            cols = slice(h * head, (h + 1) * head)
            mine = frag_v == h
            old_m, old_a, old_w = mom[at, cols], anc[at, cols], wf[at, cols]
            moment_next = outer_pull * old_m + average
            anchor_next = old_a - outer_rate * (average + outer_pull * moment_next)
            mom[at, cols] = jnp.where(mine, moment_next, old_m)
            anc[at, cols] = jnp.where(mine, anchor_next, old_a)
            mixed = blend_share * anchor_next + (1.0 - blend_share) * old_w
            start = jnp.where(mine & (flag_v == 0), mixed, old_w)
            wf[at, cols] = start
            wb[h, pl.ds(pl.multiple_of(q * blk + i * step_rows, step_rows), step_rows), :] = start.astype(jnp.bfloat16)
        return 0

    lax.fori_loop(0, blk // step_rows, outer, 0)
    w_copies = []
    for c in range(chunks):
        own = wb.at[c, pl.ds(pl.multiple_of(q * blk, 128), blk)]
        for e in range(1, quads):
            copy = remote(own, own, w_ss.at[c, e - 1], w_rs.at[c, e - 1], to_quad(e))
            copy.start()
            sent.append(copy)
    outs = []

    def put(src, dst):
        copy = pltpu.make_async_copy(src, dst, out_sem.at[len(outs)])
        copy.start()
        outs.append(copy)

    put(anc, anchor_o)
    put(mom, moment_o)

    key_scale = 1.0 / math.sqrt(width)
    grad_scale = 1.0 / math.sqrt(rows * n_fsdp)

    def rows_of(p):
        return pl.ds(pl.multiple_of(p * rows, 128), rows)

    def keys_of(c):
        for e in range(1, quads):
            at = wb.at[c, pl.ds(pl.multiple_of(quad(quads - e) * blk, 128), blk)]
            remote(at, at, w_ss.at[c, e - 1], w_rs.at[c, e - 1], to_quad(e)).wait_recv()
        for d in (1, 2, 3, 0):
            p = member(d)
            if c == 0 and d:
                for k in range(ROW_PARTS):
                    for j in range(quads):
                        at = tok.at[pl.ds(pl.multiple_of(p * rows + k * part, 16), part), pl.ds(j * blk, blk)]
                        remote(
                            at, at, t_ss.at[k, GROUP - d - 1, j], t_rs.at[k, GROUP - d - 1, j], to_member(d)
                        ).wait_recv()
            kp[c, d] = jnp.dot(tok[rows_of(p), :], wb[c], preferred_element_type=jnp.float32)
            if d:
                copy = remote(kp.at[c, d], kin.at[c, d - 1], k_ss.at[c, d - 1], k_rs.at[c, d - 1], to_member(d))
                copy.start()
                sent.append(copy)

    def residual_of(c):
        if c == 0:
            more[4].wait()
        for d in range(1, GROUP):
            remote(kp.at[c, d], kin.at[c, d - 1], k_ss.at[c, d - 1], k_rs.at[c, d - 1], to_member(d)).wait_recv()
        for i in range(rows // 128):
            at = slice(i * 128, (i + 1) * 128)
            keys = kp[c, 0, at, :]
            for d in range(1, GROUP):
                keys = keys + kin[c, d - 1, at, :]
            wide = keys * key_scale - tgt[at, c * head:(c + 1) * head].astype(jnp.float32)
            rbuf[c, :, pl.ds(pl.multiple_of(my_rows + i * 128, 128), 128)] = wide.T.astype(jnp.bfloat16)
        own = rbuf.at[c, :, rows_of(g)]
        for d in range(1, GROUP):
            copy = remote(own, own, r_ss.at[c, d - 1], r_rs.at[c, d - 1], to_member(d))
            copy.start()
            sent.append(copy)

    tile = tile_of(blk, 256)

    def grad_of(c):
        for d in range(1, GROUP):
            at = rbuf.at[c, :, rows_of(member(GROUP - d))]
            remote(at, at, r_ss.at[c, d - 1], r_rs.at[c, d - 1], to_member(d)).wait_recv()
        for e in list(range(1, quads)) + [0]:
            j = quad(e)

            def piece(i, _, j=j, e=e):
                cols = pl.ds(pl.multiple_of(j * blk + i * tile, tile), tile)
                gbuf[c, e, :, pl.ds(pl.multiple_of(i * tile, tile), tile)] = jnp.dot(
                    rbuf[c], tok[:, cols], preferred_element_type=jnp.float32
                )
                return 0

            lax.fori_loop(0, blk // tile, piece, 0)
            if e:
                copy = remote(gbuf.at[c, e], gin.at[c, e - 1], g_ss.at[c, e - 1], g_rs.at[c, e - 1], to_quad(e))
                copy.start()
                sent.append(copy)

    def finish(c):
        if c == 0:
            more[5].wait()
            more[6].wait()
        for e in range(1, quads):
            remote(gbuf.at[c, e], gin.at[c, e - 1], g_ss.at[c, e - 1], g_rs.at[c, e - 1], to_quad(e)).wait_recv()
        cols = slice(c * head, (c + 1) * head)

        def piece(i, _):
            at = pl.ds(pl.multiple_of(i * 128, 128), 128)
            total = gbuf[c, 0, :, at]
            for e in range(1, quads):
                total = total + gin[c, e - 1, :, at]
            grad = total.T * grad_scale
            stepped, mean_next, var_next = adam_update(wf[at, cols], grad, mean[at, cols], var[at, cols])
            mean[at, cols] = mean_next
            var[at, cols] = var_next
            mixed = blend_share * anc[at, cols] + (1.0 - blend_share) * stepped
            shape = (128, head)
            late = (jnp.full(shape, frag, jnp.int32) == c) & (jnp.full(shape, flag, jnp.int32) == 1)
            wf[at, cols] = jnp.where(late, mixed, stepped)
            return 0

        lax.fori_loop(0, blk // 128, piece, 0)
        put(wf.at[:, cols], weights_o.at[:, cols])
        put(mean.at[:, cols], mean_o.at[:, cols])
        put(var.at[:, cols], var_o.at[:, cols])

    keys_of(0)
    for c in range(chunks):
        residual_of(c)
        if c + 1 < chunks:
            keys_of(c + 1)
        grad_of(c)
        if c >= 2:
            finish(c - 2)
    for c in range(max(chunks - 2, 0), chunks):
        finish(c)
    for copy in sent:
        copy.wait_send()
    for copy in outs:
        copy.wait()


def on_device(n_rep, n_fsdp, tokens_in, targets, weights, adam_mean, adam_var, anchor, outer_momentum, pseudo_grad, fragment, delay):
    rows, width = tokens_in.shape[1:]
    blk, kw = weights.shape[1:]
    head = pseudo_grad.shape[2]
    chunks = kw // head
    quads = n_fsdp // GROUP
    f32, bf16 = jnp.float32, jnp.bfloat16
    state = jax.ShapeDtypeStruct((blk, kw), f32)
    hbm = pl.BlockSpec(memory_space=pl.ANY)
    smem = pl.BlockSpec(memory_space=pltpu.SMEM)
    dma = pltpu.SemaphoreType.DMA
    out = pl.pallas_call(
        functools.partial(kernel, n_rep, n_fsdp),
        out_shape=[state] * 5,
        in_specs=[smem] * 2 + [hbm] * 8,
        out_specs=[hbm] * 5,
        scratch_shapes=[
            pltpu.VMEM((rows, width), bf16),
            pltpu.VMEM((GROUP * rows, quads * blk), bf16),
            pltpu.VMEM((rows, kw), bf16),
            pltpu.VMEM((blk, kw), f32),
            pltpu.VMEM((chunks, quads * blk, head), bf16),
            pltpu.VMEM((blk, kw), f32),
            pltpu.VMEM((blk, kw), f32),
            pltpu.VMEM((blk, kw), f32),
            pltpu.VMEM((blk, kw), f32),
            pltpu.VMEM((n_rep, blk, head), f32),
            pltpu.VMEM((chunks, GROUP, rows, head), f32),
            pltpu.VMEM((chunks, GROUP - 1, rows, head), f32),
            pltpu.VMEM((chunks, head, GROUP * rows), bf16),
            pltpu.VMEM((chunks, quads, head, blk), f32),
            pltpu.VMEM((chunks, quads - 1, head, blk), f32),
            dma((7,)), dma((ROW_PARTS,)), dma((2 + 3 * chunks,)),
            dma((n_rep - 1,)), dma((n_rep - 1,)),
            dma((ROW_PARTS, GROUP - 1, quads)), dma((ROW_PARTS, GROUP - 1, quads)),
            dma((chunks, quads - 1)), dma((chunks, quads - 1)),
            dma((chunks, GROUP - 1)), dma((chunks, GROUP - 1)),
            dma((chunks, GROUP - 1)), dma((chunks, GROUP - 1)),
            dma((chunks, quads - 1)), dma((chunks, quads - 1)),
        ],
        compiler_params=pltpu.CompilerParams(
            collective_id=0, has_side_effects=True, vmem_limit_bytes=60 * 2**20
        ),
        cost_estimate=pl.CostEstimate(
            flops=4 * rows * width * kw, bytes_accessed=2 * rows * width + 40 * blk * kw, transcendentals=blk * kw
        ),
    )(
        fragment.reshape(1), delay, tokens_in[0], targets[0], weights[0], adam_mean[0], adam_var[0],
        anchor, outer_momentum, pseudo_grad[0],
    )
    return (out[0][None], out[1][None], out[2][None], out[3], out[4])


def solution(mesh):
    split = P("replica", "fsdp", None)
    return jax.shard_map(
        functools.partial(on_device, mesh.shape["replica"], mesh.shape["fsdp"]),
        mesh=mesh,
        in_specs=(split,) * 5 + (P("fsdp", None),) * 2 + (split, P(), P("replica")),
        out_specs=(split,) * 3 + (P("fsdp", None),) * 2,
        check_vma=False,
    )
```

```python
import functools
import math

import jax
import jax.numpy as jnp
from jax import lax
from jax.experimental import pallas as pl
from jax.experimental.pallas import tpu as pltpu
from jax.sharding import PartitionSpec as P

beta_first = 0.9
beta_second = 0.95
adam_epsilon = 1e-08
adam_steps = 20.0
inner_rate = 0.1
weight_decay = 0.1
outer_rate = 0.7
outer_pull = 0.9
blend_share = 0.5
norm_epsilon = 1e-05

GROUP = 4
ROW_PARTS = 4
MESH = pl.DeviceIdType.MESH


def adam_update(start_field, grad, first, second):
    mean_next = beta_first * first + (1.0 - beta_first) * grad
    var_next = beta_second * second + (1.0 - beta_second) * grad * grad
    first_fix = 1.0 - beta_first**adam_steps
    second_fix = 1.0 - beta_second**adam_steps
    ratio = mean_next / first_fix / (jnp.sqrt(var_next / second_fix) + adam_epsilon)
    return (start_field - inner_rate * (ratio + weight_decay * start_field), mean_next, var_next)


def tile_of(extent, most):
    tile = min(extent, most)
    while extent % tile:
        tile //= 2
    return tile


def coded(values):
    top = values.astype(jnp.bfloat16)
    wide = top.astype(jnp.float32)
    rest = (values - wide) * (512.0 / jnp.maximum(jnp.abs(wide), 1e-30))
    digit = jnp.clip(jnp.floor(rest), -2.0, 1.0) + 2.0
    n = values.shape[0] // 4
    low = digit[:n] * 64.0 + digit[n:2 * n] * 16.0 + digit[2 * n:3 * n] * 4.0 + digit[3 * n:] - 128.0
    return top, low.astype(jnp.bfloat16)


def decoded(top, low):
    wide = top.astype(jnp.float32)
    left = low.astype(jnp.float32) + 128.0
    digits = []
    for unit in (64.0, 16.0, 4.0):
        digit = jnp.floor(left * (1.0 / unit))
        left = left - unit * digit
        digits.append(digit)
    digits.append(left)
    digit = jnp.concatenate(digits, axis=0)
    return wide + jnp.abs(wide) * ((digit - 1.5) * (1.0 / 512.0))


def kernel(
    n_rep, n_fsdp,
    frag_ref, delay_ref, tokens_h, targets_h, weights_h, mean_h, var_h, anchor_h, moment_h, pg_h,
    weights_o, mean_o, var_o, anchor_o, moment_o,
    tin, tok, tgt, wf, wb, mean, var, anc, mom, pgs, kp, kin, rbuf, gown, gbuf, gin,
    load_sem, tload_sem, out_sem,
    pg_ss, pg_rs, t_ss, t_rs, w_ss, w_rs, k_ss, k_rs, r_ss, r_rs, g_ss, g_rs,
):
    rows, width = tin.shape
    blk, kw = wf.shape
    head = pgs.shape[2]
    chunks = kw // head
    quads = n_fsdp // GROUP
    part = rows // ROW_PARTS
    me = lax.axis_index("fsdp")
    rep = lax.axis_index("replica")
    g = lax.rem(me, GROUP)
    q = lax.div(me, GROUP)

    x = lax.rem(g, 2)
    places = (g, g + 1 - 2 * x, lax.rem(g + 2, GROUP), lax.rem(g + 3 - 2 * x, GROUP))

    def member(d):
        return lax.rem(g + d, GROUP)

    def quad(e):
        return lax.rem(q + e, quads)

    def to_member(d):
        return (rep, q * GROUP + member(d))

    def to_place(i):
        return (rep, q * GROUP + places[i])

    def to_quad(e):
        return (rep, quad(e) * GROUP + g)

    def to_replica(d):
        return (lax.rem(rep + d, n_rep), me)

    def remote(src, dst, ss, rs, where):
        return pltpu.make_async_remote_copy(
            src_ref=src, dst_ref=dst, send_sem=ss, recv_sem=rs, device_id=where, device_id_type=MESH
        )

    loads = []
    for k in range(ROW_PARTS):
        span = pl.ds(k * part, part)
        loads.append(pltpu.make_async_copy(tokens_h.at[span], tin.at[span], tload_sem.at[k]))
        loads[-1].start()
    pairs = [
        (pg_h, pgs.at[rep]), (weights_h, wf), (anchor_h, anc), (moment_h, mom),
        (targets_h, tgt), (mean_h, mean), (var_h, var),
    ]
    more = []
    for i, (src, dst) in enumerate(pairs):
        more.append(pltpu.make_async_copy(src, dst, load_sem.at[i]))
        more[-1].start()

    peers = [to_replica(d) for d in range(1, n_rep)]
    peers += [to_member(d) for d in range(1, GROUP)]
    peers += [to_quad(e) for e in range(1, quads)]
    barrier = pltpu.get_barrier_semaphore()
    for where in peers:
        pl.semaphore_signal(barrier, inc=1, device_id=where, device_id_type=MESH)
    pl.semaphore_wait(barrier, len(peers))

    sent = []

    more[0].wait()
    pg_copies = []
    for d in range(1, n_rep):
        copy = remote(pgs.at[rep], pgs.at[rep], pg_ss.at[d - 1], pg_rs.at[d - 1], to_replica(d))
        copy.start()
        sent.append(copy)
        source = lax.rem(rep + n_rep - d, n_rep)
        pg_copies.append(
            remote(pgs.at[source], pgs.at[source], pg_ss.at[d - 1], pg_rs.at[d - 1], to_replica(d))
        )

    my_rows = pl.multiple_of(g * rows, 128)
    lane = 128
    def send_tokens(k):
        loads[k].wait()

        def norm(i, _):
            at = pl.ds(pl.multiple_of(k * part + i * 16, 16), 16)
            total = jnp.zeros((16, lane), jnp.float32)
            for j in range(width // lane):
                v = tin[at, j * lane:(j + 1) * lane].astype(jnp.float32)
                total = total + v * v
            stat = jnp.sum(total, axis=-1, keepdims=True) * (1.0 / width)
            scale = jnp.broadcast_to(lax.rsqrt(stat + norm_epsilon), (16, lane))
            for j in range(width // lane):
                cols = slice(j * lane, (j + 1) * lane)
                tin[at, cols] = (tin[at, cols].astype(jnp.float32) * scale).astype(jnp.bfloat16)
            return 0

        lax.fori_loop(0, part // 16, norm, 0)
        span = pl.ds(k * part, part)
        dst_rows = pl.ds(pl.multiple_of(my_rows + k * part, 16), part)
        for d in range(1, GROUP):
            for j in range(quads):
                cols = pl.ds(pl.multiple_of((j * GROUP + member(d)) * blk, 128), blk)
                copy = remote(
                    tin.at[span, cols], tok.at[dst_rows, pl.ds(j * blk, blk)],
                    t_ss.at[k, d - 1, j], t_rs.at[k, d - 1, j], to_member(d),
                )
                copy.start()
                sent.append(copy)
        for j in range(quads):
            cols = pl.ds(pl.multiple_of((j * GROUP + g) * blk, 128), blk)
            tok[dst_rows, j * blk:(j + 1) * blk] = tin[span, cols]

    for k in range(ROW_PARTS // 2):
        send_tokens(k)

    for copy in more[1:4]:
        copy.wait()
    for copy in pg_copies:
        copy.wait_recv()
    frag = frag_ref[0]
    flag = delay_ref[0]
    step_rows = tile_of(blk, 128)

    def outer(i, _):
        at = pl.ds(pl.multiple_of(i * step_rows, step_rows), step_rows)
        shape = (step_rows, head)
        total = pgs[0, at, :]
        for r in range(1, n_rep):
            total = total + pgs[r, at, :]
        average = total / n_rep
        frag_v = jnp.full(shape, frag, jnp.int32)
        flag_v = jnp.full(shape, flag, jnp.int32)
        for h in range(chunks):
            cols = slice(h * head, (h + 1) * head)
            mine = frag_v == h
            old_m, old_a, old_w = mom[at, cols], anc[at, cols], wf[at, cols]
            moment_next = outer_pull * old_m + average
            anchor_next = old_a - outer_rate * (average + outer_pull * moment_next)
            mom[at, cols] = jnp.where(mine, moment_next, old_m)
            anc[at, cols] = jnp.where(mine, anchor_next, old_a)
            mixed = blend_share * anchor_next + (1.0 - blend_share) * old_w
            start = jnp.where(mine & (flag_v == 0), mixed, old_w)
            wf[at, cols] = start
            wb[h, pl.ds(pl.multiple_of(q * blk + i * step_rows, step_rows), step_rows), :] = start.astype(jnp.bfloat16)
        return 0

    lax.fori_loop(0, blk // step_rows, outer, 0)
    w_copies = []
    for c in range(chunks):
        own = wb.at[c, pl.ds(pl.multiple_of(q * blk, 128), blk)]
        for e in range(1, quads):
            copy = remote(own, own, w_ss.at[c, e - 1], w_rs.at[c, e - 1], to_quad(e))
            copy.start()
            sent.append(copy)
    for k in range(ROW_PARTS // 2, ROW_PARTS):
        send_tokens(k)
    outs = []

    def put(src, dst):
        copy = pltpu.make_async_copy(src, dst, out_sem.at[len(outs)])
        copy.start()
        outs.append(copy)

    put(anc, anchor_o)
    put(mom, moment_o)

    key_scale = 1.0 / math.sqrt(width)
    grad_scale = 1.0 / math.sqrt(rows * n_fsdp)

    def rows_of(p):
        return pl.ds(pl.multiple_of(p * rows, 128), rows)

    def exchange(src, dst, ss, rs, c, i, place):
        return remote(src, dst, ss.at[c, i], rs.at[c, i], to_place(place))

    def start(copy):
        copy.start()
        sent.append(copy)

    def key_parts(c):
        for e in range(1, quads):
            at = wb.at[c, pl.ds(pl.multiple_of(quad(quads - e) * blk, 128), blk)]
            remote(at, at, w_ss.at[c, e - 1], w_rs.at[c, e - 1], to_quad(e)).wait_recv()
        if c == 0:
            for d in range(1, GROUP):
                for k in range(ROW_PARTS):
                    for j in range(quads):
                        at = tok.at[pl.ds(pl.multiple_of(member(d) * rows + k * part, 16), part), pl.ds(j * blk, blk)]
                        remote(
                            at, at, t_ss.at[k, GROUP - d - 1, j], t_rs.at[k, GROUP - d - 1, j], to_member(d)
                        ).wait_recv()
        for i in (3, 1, 2, 0):
            kp[c, i] = jnp.dot(tok[rows_of(places[i]), :], wb[c], preferred_element_type=jnp.float32)

    def key_copy(c, i):
        return exchange(kp.at[c, (3, 1, 2)[i]], kin.at[c, i], k_ss, k_rs, c, i, (1, 1, 2)[i])

    def send_keys(c):
        for i in range(2):
            start(key_copy(c, i))

    def pass_keys(c):
        key_copy(c, 0).wait_recv()
        kp[c, 2] = kp[c, 2] + kin[c, 0]
        start(key_copy(c, 2))

    def residual_copy(c, i, arrived=False):
        at = rows_of(places[(2, 1, 3)[i] if arrived else (0, 0, 2)[i]])
        return exchange(rbuf.at[c, :, at], rbuf.at[c, :, at], r_ss, r_rs, c, i, (2, 1, 1)[i])

    def residual_of(c):
        if c == 0:
            more[4].wait()
        key_copy(c, 1).wait_recv()
        key_copy(c, 2).wait_recv()
        for i in range(rows // 128):
            at = slice(i * 128, (i + 1) * 128)
            keys = kp[c, 0, at, :] + kin[c, 1, at, :] + kin[c, 2, at, :]
            wide = keys * key_scale - tgt[at, c * head:(c + 1) * head].astype(jnp.float32)
            rbuf[c, :, pl.ds(pl.multiple_of(my_rows + i * 128, 128), 128)] = wide.T.astype(jnp.bfloat16)
        for i in range(2):
            start(residual_copy(c, i))

    def pass_residual(c):
        residual_copy(c, 0, True).wait_recv()
        start(residual_copy(c, 2))

    tile = tile_of(blk, 256)

    def grad_copy(c, e):
        return remote(gbuf.at[c, e - 1], gin.at[c, e - 1], g_ss.at[c, e - 1], g_rs.at[c, e - 1], to_quad(e))

    def grad_of(c):
        for i in (1, 2):
            residual_copy(c, i, True).wait_recv()
        for e in list(range(1, quads)) + [0]:
            j = quad(e)

            def piece(i, _, j=j, e=e):
                cols = pl.ds(pl.multiple_of(j * blk + i * tile, tile), tile)
                at = pl.ds(pl.multiple_of(i * tile, tile), tile)
                value = jnp.dot(rbuf[c], tok[:, cols], preferred_element_type=jnp.float32)
                if e:
                    top, low = coded(value)
                    gbuf[c, e - 1, :head, at] = top
                    gbuf[c, e - 1, head:, at] = low
                else:
                    gown[c, :, at] = value
                return 0

            lax.fori_loop(0, blk // tile, piece, 0)
            if e:
                start(grad_copy(c, e))

    def finish(c):
        if c == 0:
            more[5].wait()
            more[6].wait()
        for e in range(1, quads):
            grad_copy(c, e).wait_recv()
        cols = slice(c * head, (c + 1) * head)

        def piece(i, _):
            at = pl.ds(pl.multiple_of(i * 128, 128), 128)
            total = gown[c, :, at]
            for e in range(1, quads):
                total = total + decoded(gin[c, e - 1, :head, at], gin[c, e - 1, head:, at])
            grad = total.T * grad_scale
            stepped, mean_next, var_next = adam_update(wf[at, cols], grad, mean[at, cols], var[at, cols])
            mean[at, cols] = mean_next
            var[at, cols] = var_next
            mixed = blend_share * anc[at, cols] + (1.0 - blend_share) * stepped
            shape = (128, head)
            late = (jnp.full(shape, frag, jnp.int32) == c) & (jnp.full(shape, flag, jnp.int32) == 1)
            wf[at, cols] = jnp.where(late, mixed, stepped)
            return 0

        lax.fori_loop(0, blk // 128, piece, 0)
        put(wf.at[:, cols], weights_o.at[:, cols])
        put(mean.at[:, cols], mean_o.at[:, cols])
        put(var.at[:, cols], var_o.at[:, cols])

    key_parts(0)
    send_keys(0)
    if chunks > 1:
        key_parts(1)
    pass_keys(0)
    if chunks > 1:
        send_keys(1)
    for c in range(chunks):
        residual_of(c)
        if 0 < c < chunks - 1:
            pass_keys(c + 1)
        pass_residual(c)
        if c == 0:
            grad_of(c)
            if chunks > 1:
                pass_keys(c + 1)
        if c + 2 < chunks:
            key_parts(c + 2)
            send_keys(c + 2)
        if c:
            grad_of(c)
    for c in range(chunks):
        finish(c)
    for copy in sent:
        copy.wait_send()
    for copy in outs:
        copy.wait()


def on_device(n_rep, n_fsdp, tokens_in, targets, weights, adam_mean, adam_var, anchor, outer_momentum, pseudo_grad, fragment, delay):
    rows, width = tokens_in.shape[1:]
    blk, kw = weights.shape[1:]
    head = pseudo_grad.shape[2]
    chunks = kw // head
    quads = n_fsdp // GROUP
    f32, bf16 = jnp.float32, jnp.bfloat16
    state = jax.ShapeDtypeStruct((blk, kw), f32)
    hbm = pl.BlockSpec(memory_space=pl.ANY)
    smem = pl.BlockSpec(memory_space=pltpu.SMEM)
    dma = pltpu.SemaphoreType.DMA
    out = pl.pallas_call(
        functools.partial(kernel, n_rep, n_fsdp),
        out_shape=[state] * 5,
        in_specs=[smem] * 2 + [hbm] * 8,
        out_specs=[hbm] * 5,
        scratch_shapes=[
            pltpu.VMEM((rows, width), bf16),
            pltpu.VMEM((GROUP * rows, quads * blk), bf16),
            pltpu.VMEM((rows, kw), bf16),
            pltpu.VMEM((blk, kw), f32),
            pltpu.VMEM((chunks, quads * blk, head), bf16),
            pltpu.VMEM((blk, kw), f32),
            pltpu.VMEM((blk, kw), f32),
            pltpu.VMEM((blk, kw), f32),
            pltpu.VMEM((blk, kw), f32),
            pltpu.VMEM((n_rep, blk, head), f32),
            pltpu.VMEM((chunks, GROUP, rows, head), f32),
            pltpu.VMEM((chunks, GROUP - 1, rows, head), f32),
            pltpu.VMEM((chunks, head, GROUP * rows), bf16),
            pltpu.VMEM((chunks, head, blk), f32),
            pltpu.VMEM((chunks, quads - 1, head * 5 // 4, blk), bf16),
            pltpu.VMEM((chunks, quads - 1, head * 5 // 4, blk), bf16),
            dma((7,)), dma((ROW_PARTS,)), dma((2 + 3 * chunks,)),
            dma((n_rep - 1,)), dma((n_rep - 1,)),
            dma((ROW_PARTS, GROUP - 1, quads)), dma((ROW_PARTS, GROUP - 1, quads)),
            dma((chunks, quads - 1)), dma((chunks, quads - 1)),
            dma((chunks, GROUP - 1)), dma((chunks, GROUP - 1)),
            dma((chunks, GROUP - 1)), dma((chunks, GROUP - 1)),
            dma((chunks, quads - 1)), dma((chunks, quads - 1)),
        ],
        compiler_params=pltpu.CompilerParams(
            collective_id=0, has_side_effects=True, vmem_limit_bytes=60 * 2**20
        ),
        cost_estimate=pl.CostEstimate(
            flops=4 * rows * width * kw, bytes_accessed=2 * rows * width + 40 * blk * kw, transcendentals=blk * kw
        ),
    )(
        fragment.reshape(1), delay, tokens_in[0], targets[0], weights[0], adam_mean[0], adam_var[0],
        anchor, outer_momentum, pseudo_grad[0],
    )
    return (out[0][None], out[1][None], out[2][None], out[3], out[4])


def solution(mesh):
    split = P("replica", "fsdp", None)
    return jax.shard_map(
        functools.partial(on_device, mesh.shape["replica"], mesh.shape["fsdp"]),
        mesh=mesh,
        in_specs=(split,) * 5 + (P("fsdp", None),) * 2 + (split, P(), P("replica")),
        out_specs=(split,) * 3 + (P("fsdp", None),) * 2,
        check_vma=False,
    )
```
